128 devices in a mesh: tile: 32 (over z, x, core), group: 4 (over y).
Axes of the slice: x: 4, y: 4, z: 4, core: 2. Of those that a mesh axis runs over, the one named last changes fastest.
Arguments:
- latent: bfloat16 [16, 64, 160, 384], P('group', 'tile'), may hold values from -6 to 6
- tile_rows: int32 [32], replicated, may hold values from 1 to 2, 56 in all
- gain_first: float32 [384], replicated, may hold values from 0.1 to 1.9
- kernel_first: bfloat16 [3, 3, 3, 384, 384], replicated, may hold values from -0.0625 to 0.0625
- gain_second: float32 [384], replicated, may hold values from 0.1 to 1.9
- kernel_second: bfloat16 [3, 3, 3, 384, 384], replicated, may hold values from -0.0625 to 0.0625
Outputs:
- decoded: bfloat16 [16, 64, 160, 384], P('group', 'tile')
The draws below stay inside these ranges and needn't reach their ends.
Inputs may be any that keep to these rules, and one draw needn't show every extreme that they name: tile_rows sum to 56.
All inputs are finite; a program needn't handle non-finite values.
Results may differ from the reference program's by a relative error of at most 0.004.
Values may be sent and summed in bfloat16 or wider, within the bound.
A program may use at most 256 MiB of HBM per device.

```python
import math
import jax
import jax.numpy as jnp
import numpy as np
from jax import lax

C = 384
W = 160
ROWS_DEV = 2
HEIGHT = 64
FRAMES = 16
LIVE_ROWS = 56
N_TILE = 32


def block_levels(own_key, shape, pieces, smallest, high):
    def one(position, parts):
        draws = jax.random.uniform(jax.random.fold_in(jax.random.fold_in(own_key, 6), position), (parts,), jnp.float32, smallest / len(pieces), high / len(pieces))
        return jnp.repeat(jnp.exp(draws), shape[position] // parts).reshape((-1,) + (1,) * (len(shape) - position - 1))

    level = one(*pieces[0])
    for cut in pieces[1:]:
        level = level * one(*cut)
    return level


def split_up(count, total, reach, skew):
    weights = [(1 << 20) // math.isqrt(standing ** skew) + 1 for standing in range(2, count + 1)]
    rest, given = total - reach - (count - 1), [1] * (count - 1)
    while rest > 0:
        movable = [i for i in range(count - 1) if given[i] < reach]
        pool, budget = sum([weights[i] for i in movable]), rest
        for i in movable:
            addition = min(reach - given[i], max(1, budget * weights[i] // pool), rest)
            given[i] = given[i] + addition
            rest = rest - addition
    return np.array([reach] + given)


def ragged_sizes(rng, amount, total, reach, skew):
    if amount == 2:
        one = jax.random.randint(rng, (), max(1, total - reach), min(reach, total - 1) + 1)
        return jnp.stack([one, total - one])
    tallies = jnp.asarray(split_up(amount, total, reach, skew), jnp.int32)
    couples = (amount - 1) // 2
    donor, taker = tallies[1:1 + 2 * couples:2], tallies[2:2 + 2 * couples:2]
    room = jnp.minimum(donor - 1, reach - taker)
    shifted = jax.random.randint(jax.random.fold_in(rng, 1), (couples,), 0, 1 << 20) % (room + 1)
    tallies = tallies.at[1:1 + 2 * couples:2].set(donor - shifted).at[2:2 + 2 * couples:2].set(taker + shifted)
    return tallies[jax.random.permutation(jax.random.fold_in(rng, 2), amount)]


def scatter_about(stream_key, dims, scale, limit, cuts=(), kind=jnp.bfloat16):
    entries = jax.random.normal(stream_key, dims, jnp.float32) * scale
    if len(cuts) > 0:
        entries = block_levels(stream_key, dims, cuts, -0.22, 0.18) * entries
    return jnp.clip(entries, min=-limit, max=limit).astype(kind)


def setup_inputs(seed: int = 0) -> dict:
    splits = jax.random.split(jax.random.key(seed), 7)
    return {
        "latent": scatter_about(splits[0], (FRAMES, HEIGHT, W, C), 1.0, 6.0, ((0, 4), (1, 32))),
        "tile_rows": ragged_sizes(splits[1], N_TILE, LIVE_ROWS, ROWS_DEV, 2).astype(jnp.int32),
        "gain_first": jnp.clip(1.0 + 0.18 * jax.random.normal(splits[2], (C,), jnp.float32), 0.1, 1.9),
        "kernel_first": scatter_about(splits[3], (3, 3, 3, C, C), (27 * C) ** -0.5, 0.0625),
        "gain_second": jnp.clip(1.0 + 0.18 * jax.random.normal(splits[4], (C,), jnp.float32), 0.1, 1.9),
        "kernel_second": scatter_about(splits[5], (3, 3, 3, C, C), (27 * C) ** -0.5, 0.0625),
    }


def activate(values, gain, row_mask):
    values = values.astype(jnp.float32)
    scale = jax.lax.rsqrt(lax.optimization_barrier(jnp.mean(values * values, axis=-1, keepdims=True)) + 1e-06)
    return jax.nn.silu(values * scale * gain) * row_mask

def convolve(padded, kernel, out_frames, out_rows, columns):
    padded_w = jnp.pad(padded, ((0, 0), (0, 0), (1, 1), (0, 0)))
    channels = kernel.shape[3]
    summed = jnp.zeros((out_frames, out_rows, columns, kernel.shape[4]), jnp.float32)
    for tap_time in range(3):
        for tap_row in range(3):
            slab = padded_w[tap_time:tap_time + out_frames, tap_row:tap_row + out_rows]
            stacked = jnp.concatenate([slab[:, :, tap_col:tap_col + columns] for tap_col in range(3)], axis=-1)
            matrix = kernel[tap_time, tap_row].reshape(3 * channels, kernel.shape[4])
            summed = summed + jnp.einsum('fhwc,cd->fhwd', stacked, matrix, preferred_element_type=jnp.float32)
    return summed

def reference(latent, tile_rows, gain_first, kernel_first, gain_second, kernel_second):
    frames, height, columns, channels = latent.shape
    rows = jnp.arange(height, dtype=jnp.int32)
    live = jnp.take(tile_rows, rows // ROWS_DEV)
    row_mask = (rows % ROWS_DEV < live).astype(jnp.float32)[None, :, None, None]
    first = activate(latent, gain_first, row_mask).astype(jnp.bfloat16)
    padded = jnp.pad(first, ((2, 0), (1, 1), (0, 0), (0, 0)))
    hidden = convolve(padded, kernel_first, frames, height, columns)
    second = activate(hidden, gain_second, row_mask).astype(jnp.bfloat16)
    padded = jnp.pad(second, ((2, 0), (1, 1), (0, 0), (0, 0)))
    branch = convolve(padded, kernel_second, frames, height, columns)
    return ((latent.astype(jnp.float32) + branch) * row_mask).astype(jnp.bfloat16)
```

```python
import functools

import jax
import jax.numpy as jnp
from jax import lax
from jax.experimental import pallas as pl
from jax.experimental.pallas import tpu as pltpu
from jax.sharding import PartitionSpec as P

MESH = pl.DeviceIdType.MESH
cat = jnp.concatenate
F32 = jnp.float32
BF16 = jnp.bfloat16


def activate(values, gain, live):
    scale = lax.rsqrt(jnp.mean(values * values, axis=-1, keepdims=True) + 1e-06)
    u = values * scale * gain
    return (u / (1.0 + jnp.exp(-u))) * live


def shift_sum(before, here, after):
    columns = here.shape[0]
    place = lax.broadcasted_iota(jnp.int32, here.shape, 0)
    left = jnp.where(place == 0, 0.0, pltpu.roll(before, 1, 0))
    right = jnp.where(place == columns - 1, 0.0, pltpu.roll(after, columns - 1, 0))
    return left + here + right


def own_rows(x, w, frame, tap):
    _, _, columns, channels = x.shape
    lhs = cat([x[frame + tap : frame + tap + 2, r].reshape(2 * columns, channels) for r in (1, 2)], axis=1)
    rhs = cat([cat([w[tap, r - out, l] for out in (0, 1) for l in range(3)], axis=1) for r in (1, 2)], axis=0)
    return jnp.dot(lhs, rhs, preferred_element_type=F32)


def halo_row(x, w, frame, out):
    _, _, columns, channels = x.shape
    lhs = cat([x[frame + i : frame + i + 2, 3 * out].reshape(2 * columns, channels) for i in range(3)], axis=1)
    rhs = cat([cat([w[i, 2 * out, l] for l in range(3)], axis=1) for i in range(3)], axis=0)
    return jnp.dot(lhs, rhs, preferred_element_type=F32)


def kernel(
    tiles, groups,
    latent, tile_rows, gain_first, kernel_first, gain_second, kernel_second,
    decoded,
    xa, xb, wa, wb, lat, acc, outv,
    lat_sem, w_sem, out_sem, send_y, recv_y, send_r, recv_r,
):
    frames, rows, columns, channels = lat.shape
    tile = lax.axis_index("tile")
    group = lax.axis_index("group")
    up = lax.rem(tile + tiles - 1, tiles)
    down = lax.rem(tile + 1, tiles)
    after = lax.rem(group + 1, groups)
    before = lax.rem(group + groups - 1, groups)

    lat_copy = [pltpu.make_async_copy(latent.at[2 * c : 2 * c + 2], lat.at[2 * c : 2 * c + 2], lat_sem.at[c]) for c in range(2)]
    wa_copy = [pltpu.make_async_copy(kernel_first.at[i], wa.at[i], w_sem.at[i]) for i in range(3)]
    wb_copy = [pltpu.make_async_copy(kernel_second.at[i], wb.at[i], w_sem.at[3 + i]) for i in range(3)]
    for copy in (lat_copy[1], lat_copy[0], *wa_copy, *wb_copy):
        copy.start()

    barrier = pltpu.get_barrier_semaphore()
    for place in ((up, group), (down, group), (tile, after), (tile, before)):
        pl.semaphore_signal(barrier, inc=1, device_id=place, device_id_type=MESH)
    pl.semaphore_wait(barrier, 4)

    live = [jnp.minimum(jnp.maximum(tile_rows[tile] - r, 0), 1).astype(F32) for r in range(rows)]

    def to_next(step, x, c):
        return pltpu.make_async_remote_copy(
            src_ref=x.at[frames + c, 1:3], dst_ref=x.at[c, 1:3],
            send_sem=send_y.at[step, c], recv_sem=recv_y.at[step, c],
            device_id=(tile, after), device_id_type=MESH,
        )

    spans = ((4, 2), (2, 2), (0, 1), (1, 1))

    def to_tile(step, x, way, c):
        at, count = spans[c]
        source, target = ((1, 3), (2, 0))[way]
        return pltpu.make_async_remote_copy(
            src_ref=x.at[at : at + count, source], dst_ref=x.at[at : at + count, target],
            send_sem=send_r.at[step, way, c], recv_sem=recv_r.at[step, way, c],
            device_id=((up, down)[way], group), device_id_type=MESH,
        )

    def rows_sent(step, x, c):
        for way in range(2):
            to_tile(step, x, way, c).start()

    def rows_here(step, x, cs):
        for c in cs:
            for way in range(2):
                to_tile(step, x, way, c).wait_recv()
        lo = min(spans[c][0] for c in cs)
        hi = max(sum(spans[c]) for c in cs)
        nothing = jnp.zeros((hi - lo, columns, channels), BF16)

        @pl.when(tile == 0)
        def _():
            x[lo:hi, 0] = nothing

        @pl.when(tile == tiles - 1)
        def _():
            x[lo:hi, 3] = nothing

    def frames_here(step, x):
        for c in range(2):
            to_next(step, x, c).wait_recv()

        @pl.when(group == 0)
        def _():
            x[0:2, 1:3] = jnp.zeros((2, 2, columns, channels), BF16)

        for c in range(2):
            rows_sent(step, x, 2 + c)

    def own(x, w, frame, wait=None):
        for tap in range(3):
            if wait is not None:
                wait[tap].wait()
            y = own_rows(x, w, frame, tap)
            for r in range(2):
                for l in range(3):
                    at = (3 * r + l) * channels
                    part = y[:, at : at + channels].reshape(2, columns, channels)
                    if tap:
                        acc[r, l] += part
                    else:
                        acc[r, l] = part

    def halo(x, w, frame):
        for r in range(2):
            y = halo_row(x, w, frame, r)
            for l in range(3):
                acc[r, l] += y[:, l * channels : (l + 1) * channels].reshape(2, columns, channels)

    def hidden(f, r):
        return shift_sum(acc[r, 0, f], acc[r, 1, f], acc[r, 2, f])

    def second(frame):
        for f in range(2):
            for r in range(2):
                xb[2 + frame + f, 1 + r] = activate(hidden(f, r), gain_second[...], live[r]).astype(BF16)

    out_copy = [pltpu.make_async_copy(outv.at[2 * c : 2 * c + 2], decoded.at[2 * c : 2 * c + 2], out_sem.at[c]) for c in range(2)]

    def finish(frame):
        for f in range(2):
            for r in range(2):
                total = lat[frame + f, r].astype(F32) + hidden(f, r)
                outv[frame + f, r] = (total * live[r]).astype(BF16)
        out_copy[frame // 2].start()

    for c in (1, 0):
        lat_copy[c].wait()
        for f in range(2 * c, 2 * c + 2):
            for r in range(2):
                xa[2 + f, 1 + r] = activate(lat[f, r].astype(F32), gain_first[...], live[r]).astype(BF16)
        if c == 1:
            for e in range(2):
                to_next(0, xa, e).start()
        rows_sent(0, xa, 1 - c)

    own(xa, wa, 2, wa_copy)
    rows_here(0, xa, (0, 1))
    halo(xa, wa, 2)
    second(2)
    for e in range(2):
        to_next(1, xb, e).start()
    rows_sent(1, xb, 0)

    frames_here(0, xa)
    own(xa, wa, 0)
    rows_here(0, xa, (2, 3))
    halo(xa, wa, 0)
    second(0)
    rows_sent(1, xb, 1)

    own(xb, wb, 2, wb_copy)
    rows_here(1, xb, (0, 1))
    halo(xb, wb, 2)
    finish(2)

    frames_here(1, xb)
    own(xb, wb, 0)
    rows_here(1, xb, (2, 3))
    halo(xb, wb, 0)
    finish(0)

    for copy in out_copy:
        copy.wait()
    for step, x in enumerate((xa, xb)):
        for e in range(2):
            to_next(step, x, e).wait_send()
        for c in range(4):
            for way in range(2):
                to_tile(step, x, way, c).wait_send()


def solution(mesh):
    tiles, groups = mesh.shape["tile"], mesh.shape["group"]

    def local(latent, tile_rows, gain_first, kernel_first, gain_second, kernel_second):
        frames, rows, columns, channels = latent.shape
        halo = (frames + 2, rows + 2, columns, channels)
        vmem = pl.BlockSpec(memory_space=pltpu.VMEM)
        away = pl.BlockSpec(memory_space=pl.ANY)
        smem = pl.BlockSpec(memory_space=pltpu.SMEM)
        dma = pltpu.SemaphoreType.DMA
        return pl.pallas_call(
            functools.partial(kernel, tiles, groups),
            out_shape=jax.ShapeDtypeStruct(latent.shape, BF16),
            in_specs=[away, smem, vmem, away, vmem, away],
            out_specs=away,
            scratch_shapes=[
                pltpu.VMEM(halo, BF16),
                pltpu.VMEM(halo, BF16),
                pltpu.VMEM(kernel_first.shape, BF16),
                pltpu.VMEM(kernel_second.shape, BF16),
                pltpu.VMEM(latent.shape, BF16),
                pltpu.VMEM((2, 3, 2, columns, channels), F32),
                pltpu.VMEM(latent.shape, BF16),
                dma((2,)),
                dma((6,)),
                dma((2,)),
                dma((2, 2)),
                dma((2, 2)),
                dma((2, 2, 4)),
                dma((2, 2, 4)),
            ],
            compiler_params=pltpu.CompilerParams(
                collective_id=0, has_side_effects=True, vmem_limit_bytes=56 * 2**20
            ),
            cost_estimate=pl.CostEstimate(
                flops=4 * 27 * frames * rows * columns * channels * channels,
                bytes_accessed=2 * (2 * latent.size + 2 * kernel_first.size),
                transcendentals=2 * latent.size,
            ),
        )(
            latent, tile_rows,
            gain_first.reshape(1, channels), kernel_first,
            gain_second.reshape(1, channels), kernel_second,
        )

    in_specs = (P("group", "tile", None, None), P(), P(), P(), P(), P())
    out_specs = P("group", "tile", None, None)
    return jax.shard_map(local, mesh=mesh, in_specs=in_specs, out_specs=out_specs, check_vma=False)
```

```python
import functools

import jax
import jax.numpy as jnp
from jax import lax
from jax.experimental import pallas as pl
from jax.experimental.pallas import tpu as pltpu
from jax.sharding import PartitionSpec as P

MESH = pl.DeviceIdType.MESH
cat = jnp.concatenate
F32 = jnp.float32
BF16 = jnp.bfloat16


def activate(values, gain, live):
    scale = lax.rsqrt(jnp.mean(values * values, axis=-1, keepdims=True) + 1e-06)
    u = values * scale * gain
    return (u / (1.0 + jnp.exp(-u))) * live


def shift_sum(before, here, after):
    columns = here.shape[0]
    place = lax.broadcasted_iota(jnp.int32, here.shape, 0)
    left = jnp.where(place == 0, 0.0, pltpu.roll(before, 1, 0))
    right = jnp.where(place == columns - 1, 0.0, pltpu.roll(after, columns - 1, 0))
    return left + here + right


def own_rows(x, w, frame, tap):
    _, _, columns, channels = x.shape
    lhs = cat([x[frame + tap : frame + tap + 2, r].reshape(2 * columns, channels) for r in (1, 2)], axis=1)
    rhs = cat([cat([w[tap, r - out, l] for out in (0, 1) for l in range(3)], axis=1) for r in (1, 2)], axis=0)
    return jnp.dot(lhs, rhs, preferred_element_type=F32)


def halo_row(x, w, frame, out, taps):
    _, _, columns, channels = x.shape
    lhs = cat([x[frame + i : frame + i + 2, 3 * out].reshape(2 * columns, channels) for i in taps], axis=1)
    rhs = cat([cat([w[i, 2 * out, l] for l in range(3)], axis=1) for i in taps], axis=0)
    return jnp.dot(lhs, rhs, preferred_element_type=F32)


def kernel(
    tiles, groups,
    latent, tile_rows, gain_first, kernel_first, gain_second, kernel_second,
    decoded,
    xa, xb, wa, wb, lat, acc, outv,
    lat_sem, w_sem, out_sem, send_y, recv_y, send_r, recv_r,
):
    frames, rows, columns, channels = lat.shape
    tile = lax.axis_index("tile")
    group = lax.axis_index("group")
    above, below = tile > 0, tile < tiles - 1
    earlier, later = group > 0, group < groups - 1
    up, down = jnp.maximum(tile - 1, 0), jnp.minimum(tile + 1, tiles - 1)
    before, after = jnp.maximum(group - 1, 0), jnp.minimum(group + 1, groups - 1)

    lat_copy = [pltpu.make_async_copy(latent.at[f], lat.at[f], lat_sem.at[f]) for f in range(frames)]
    wa_copy = [pltpu.make_async_copy(kernel_first.at[i], wa.at[i], w_sem.at[i]) for i in range(3)]
    wb_copy = [pltpu.make_async_copy(kernel_second.at[i], wb.at[i], w_sem.at[3 + i]) for i in range(3)]
    out_copy = [pltpu.make_async_copy(outv.at[f], decoded.at[f], out_sem.at[f]) for f in range(frames)]
    for copy in (*lat_copy[::-1], *wa_copy[::-1], *wb_copy[::-1]):
        copy.start()

    barrier = pltpu.get_barrier_semaphore()
    around = ((above, (up, group)), (below, (down, group)), (earlier, (tile, before)), (later, (tile, after)))
    for there, place in around:

        @pl.when(there)
        def _():
            pl.semaphore_signal(barrier, inc=1, device_id=place, device_id_type=MESH)

    live = [jnp.minimum(jnp.maximum(tile_rows[tile] - r, 0), 1).astype(F32) for r in range(rows)]
    gains = [gain_first[...].reshape(1, channels), gain_second[...].reshape(1, channels)]
    xs = (xa, xb)

    def to_next(step, e):
        x = xs[step]
        return pltpu.make_async_remote_copy(
            src_ref=x.at[frames + e, 1:3], dst_ref=x.at[e, 1:3],
            send_sem=send_y.at[step, e], recv_sem=recv_y.at[step, e],
            device_id=(tile, after), device_id_type=MESH,
        )

    def to_tile(step, way, f):
        x = xs[step]
        source, target = ((1, 3), (2, 0))[way]
        return pltpu.make_async_remote_copy(
            src_ref=x.at[f, source], dst_ref=x.at[f, target],
            send_sem=send_r.at[step, way, f], recv_sem=recv_r.at[step, way, f],
            device_id=((up, down)[way], group), device_id_type=MESH,
        )

    def along(f, there):
        return there if f >= 2 else there & earlier

    def send_rows(step, f):
        for way, there in enumerate((above, below)):

            @pl.when(along(f, there))
            def _():
                to_tile(step, way, f).start()

    def wait_rows(step, fs):
        for f in fs:
            for way, there in enumerate((below, above)):

                @pl.when(along(f, there))
                def _():
                    to_tile(step, way, f).wait_recv()

    def send_frame(step, e):
        @pl.when(later)
        def _():
            to_next(step, e).start()

    def pass_frame(step, e):
        @pl.when(earlier)
        def _():
            to_next(step, e).wait_recv()

        send_rows(step, e)

    def ready(step, f):
        if f >= frames:
            send_frame(step, f - frames)
        send_rows(step, f)

    begun = set()

    def add(pair, r, l, part, fresh):
        part = part.reshape(2, columns, channels)
        if fresh:
            acc[pair, r, l] = part
        else:
            acc[pair, r, l] += part

    def own(step, frame, tap):
        x, w, pair = xs[step], (wa, wb)[step], frame // 2
        y = own_rows(x, w, frame, tap)
        for r in range(2):
            for l in range(3):
                at = (3 * r + l) * channels
                add(pair, r, l, y[:, at : at + channels], (step, pair) not in begun)
        begun.add((step, pair))

    def halo(step, frame, taps):
        x, w, pair = xs[step], (wa, wb)[step], frame // 2
        for r in range(2):
            y = halo_row(x, w, frame, r, taps)
            for l in range(3):
                add(pair, r, l, y[:, l * channels : (l + 1) * channels], False)

    def summed(f, r):
        pair, e = divmod(f, 2)
        return shift_sum(acc[pair, r, 0, e], acc[pair, r, 1, e], acc[pair, r, 2, e])

    def second(frame):
        for f in (frame + 1, frame):
            for r in range(2):
                xb[2 + f, 1 + r] = activate(summed(f, r), gains[1], live[r]).astype(BF16)
            ready(1, 2 + f)

    def finish(frame):
        for f in (frame, frame + 1):
            for r in range(2):
                total = lat[f, r].astype(F32) + summed(f, r)
                outv[f, r] = (total * live[r]).astype(BF16)
            out_copy[f].start()

    for f in reversed(range(frames)):
        lat_copy[f].wait()
        for r in range(2):
            xa[2 + f, 1 + r] = activate(lat[f, r].astype(F32), gains[0], live[r]).astype(BF16)
        if f == frames - 1:
            count = sum(there.astype(jnp.int32) for there, _ in around)
            pl.semaphore_wait(barrier, count)
        ready(0, 2 + f)

    for x in xs:

        @pl.when(jnp.logical_not(above))
        def _():
            x[:, 0] = jnp.zeros((frames + 2, columns, channels), BF16)

        @pl.when(jnp.logical_not(below))
        def _():
            x[:, 3] = jnp.zeros((frames + 2, columns, channels), BF16)

        @pl.when(jnp.logical_not(earlier))
        def _():
            x[0:2] = jnp.zeros((2, rows + 2, columns, channels), BF16)

    for tap in (2, 1, 0):
        wa_copy[tap].wait()
        own(0, 2, tap)
    own(0, 0, 2)
    wait_rows(0, (5, 4, 3, 2))
    halo(0, 2, (0, 1, 2))
    second(2)
    pass_frame(0, 1)
    wb_copy[2].wait()
    own(1, 2, 2)
    own(0, 0, 1)
    pass_frame(0, 0)
    own(0, 0, 0)
    wait_rows(0, (1,))
    halo(0, 0, (1, 2))
    wait_rows(1, (5, 4))
    halo(1, 2, (2,))
    wait_rows(0, (0,))
    halo(0, 0, (0,))
    second(0)

    wb_copy[1].wait()
    own(1, 2, 1)
    pass_frame(1, 1)
    wb_copy[0].wait()
    own(1, 2, 0)
    own(1, 0, 2)
    own(1, 0, 1)
    wait_rows(1, (3, 2))
    halo(1, 2, (0, 1))
    finish(2)
    pass_frame(1, 0)
    own(1, 0, 0)
    wait_rows(1, (1,))
    halo(1, 0, (1, 2))
    wait_rows(1, (0,))
    halo(1, 0, (0,))
    finish(0)

    for copy in out_copy:
        copy.wait()
    for step in range(2):
        for e in range(2):

            @pl.when(later)
            def _():
                to_next(step, e).wait_send()

        for f in range(frames + 2):
            for way, there in enumerate((above, below)):

                @pl.when(along(f, there))
                def _():
                    to_tile(step, way, f).wait_send()


def solution(mesh):
    tiles, groups = mesh.shape["tile"], mesh.shape["group"]

    def local(latent, tile_rows, gain_first, kernel_first, gain_second, kernel_second):
        frames, rows, columns, channels = latent.shape
        halo = (frames + 2, rows + 2, columns, channels)
        vmem = pl.BlockSpec(memory_space=pltpu.VMEM)
        away = pl.BlockSpec(memory_space=pl.ANY)
        smem = pl.BlockSpec(memory_space=pltpu.SMEM)
        dma = pltpu.SemaphoreType.DMA
        return pl.pallas_call(
            functools.partial(kernel, tiles, groups),
            out_shape=jax.ShapeDtypeStruct(latent.shape, BF16),
            in_specs=[away, smem, vmem, away, vmem, away],
            out_specs=away,
            scratch_shapes=[
                pltpu.VMEM(halo, BF16),
                pltpu.VMEM(halo, BF16),
                pltpu.VMEM(kernel_first.shape, BF16),
                pltpu.VMEM(kernel_second.shape, BF16),
                pltpu.VMEM(latent.shape, BF16),
                pltpu.VMEM((2, 2, 3, 2, columns, channels), F32),
                pltpu.VMEM(latent.shape, BF16),
                dma((frames,)),
                dma((6,)),
                dma((frames,)),
                dma((2, 2)),
                dma((2, 2)),
                dma((2, 2, frames + 2)),
                dma((2, 2, frames + 2)),
            ],
            compiler_params=pltpu.CompilerParams(
                collective_id=0, has_side_effects=True, vmem_limit_bytes=56 * 2**20
            ),
            cost_estimate=pl.CostEstimate(
                flops=4 * 27 * frames * rows * columns * channels * channels,
                bytes_accessed=2 * (2 * latent.size + 2 * kernel_first.size),
                transcendentals=2 * latent.size,
            ),
        )(
            latent, tile_rows,
            gain_first, kernel_first,
            gain_second, kernel_second,
        )

    in_specs = (P("group", "tile", None, None), P(), P(), P(), P(), P())
    out_specs = P("group", "tile", None, None)
    return jax.shard_map(local, mesh=mesh, in_specs=in_specs, out_specs=out_specs, check_vma=False)
```

```python
import functools

import jax
import jax.numpy as jnp
from jax import lax
from jax.experimental import pallas as pl
from jax.experimental.pallas import tpu as pltpu
from jax.sharding import PartitionSpec as P

MESH = pl.DeviceIdType.MESH
cat = jnp.concatenate
F32 = jnp.float32
BF16 = jnp.bfloat16


def activate(values, gain, live):
    scale = lax.rsqrt(jnp.mean(values * values, axis=-1, keepdims=True) + 1e-06)
    u = values * scale * gain
    return (u / (1.0 + jnp.exp(-u))) * live


def shift_sum(before, here, after):
    columns = here.shape[0]
    place = lax.broadcasted_iota(jnp.int32, here.shape, 0)
    left = jnp.where(place == 0, 0.0, pltpu.roll(before, 1, 0))
    right = jnp.where(place == columns - 1, 0.0, pltpu.roll(after, columns - 1, 0))
    return left + here + right


def own_rows(x, w, frame, count, tap):
    _, _, columns, channels = x.shape
    at = frame + tap
    lhs = cat([x[at : at + count, r].reshape(count * columns, channels) for r in (1, 2)], axis=1)
    rhs = cat([cat([w[tap, r - out, l] for out in (0, 1) for l in range(3)], axis=1) for r in (1, 2)], axis=0)
    return jnp.dot(lhs, rhs, preferred_element_type=F32)


def halo_row(x, w, frame, count, out, taps):
    _, _, columns, channels = x.shape
    lhs = cat([x[frame + i : frame + i + count, 3 * out].reshape(count * columns, channels) for i in taps], axis=1)
    rhs = cat([cat([w[i, 2 * out, l] for l in range(3)], axis=1) for i in taps], axis=0)
    return jnp.dot(lhs, rhs, preferred_element_type=F32)


def kernel(
    tiles, groups,
    latent, tile_rows, gain_first, kernel_first, gain_second, kernel_second,
    decoded,
    xa, xb, wa, wb, lat, acc, outv,
    lat_sem, w_sem, out_sem, send_y, recv_y, send_r, recv_r,
):
    frames, rows, columns, channels = lat.shape
    tile = lax.axis_index("tile")
    group = lax.axis_index("group")
    above, below = tile > 0, tile < tiles - 1
    earlier, later = group > 0, group < groups - 1
    up, down = jnp.maximum(tile - 1, 0), jnp.minimum(tile + 1, tiles - 1)
    before, after = jnp.maximum(group - 1, 0), jnp.minimum(group + 1, groups - 1)

    lat_copy = [pltpu.make_async_copy(latent.at[f], lat.at[f], lat_sem.at[f]) for f in range(frames)]
    wa_copy = [pltpu.make_async_copy(kernel_first.at[i], wa.at[i], w_sem.at[i]) for i in range(3)]
    wb_copy = [pltpu.make_async_copy(kernel_second.at[i], wb.at[i], w_sem.at[3 + i]) for i in range(3)]
    out_copy = [pltpu.make_async_copy(outv.at[f], decoded.at[f], out_sem.at[f]) for f in range(frames)]
    for copy in (*lat_copy[::-1], wa_copy[2]):
        copy.start()

    barrier = pltpu.get_barrier_semaphore()
    around = ((above, (up, group)), (below, (down, group)), (earlier, (tile, before)), (later, (tile, after)))
    for there, place in around:

        @pl.when(there)
        def _():
            pl.semaphore_signal(barrier, inc=1, device_id=place, device_id_type=MESH)

    live = [jnp.minimum(jnp.maximum(tile_rows[tile] - r, 0), 1).astype(F32) for r in range(rows)]
    gains = [gain_first[...].reshape(1, channels), gain_second[...].reshape(1, channels)]
    xs = (xa, xb)

    def to_next(step, e):
        x = xs[step]
        return pltpu.make_async_remote_copy(
            src_ref=x.at[frames + e, 1:3], dst_ref=x.at[e, 1:3],
            send_sem=send_y.at[step, e], recv_sem=recv_y.at[step, e],
            device_id=(tile, after), device_id_type=MESH,
        )

    def to_tile(step, way, f):
        x = xs[step]
        source, target = ((1, 3), (2, 0))[way]
        return pltpu.make_async_remote_copy(
            src_ref=x.at[f, source], dst_ref=x.at[f, target],
            send_sem=send_r.at[step, way, f], recv_sem=recv_r.at[step, way, f],
            device_id=((up, down)[way], group), device_id_type=MESH,
        )

    def along(f, there):
        return there if f >= 2 else there & earlier

    def send_rows(step, f):
        for way, there in enumerate((above, below)):

            @pl.when(along(f, there))
            def _():
                to_tile(step, way, f).start()

    def wait_rows(step, fs):
        for f in fs:
            for way, there in enumerate((below, above)):

                @pl.when(along(f, there))
                def _():
                    to_tile(step, way, f).wait_recv()

    def send_frame(step, e):
        @pl.when(later)
        def _():
            to_next(step, e).start()

    def pass_frame(step, e):
        @pl.when(earlier)
        def _():
            to_next(step, e).wait_recv()

        send_rows(step, e)

    def ready(step, f):
        if f >= frames:
            send_frame(step, f - frames)
        send_rows(step, f)

    def add(frame, count, r, l, part, fresh):
        pair, e = divmod(frame, 2)
        part = part.reshape(count, columns, channels)
        if fresh:
            acc[pair, r, l, e : e + count] = part
        else:
            acc[pair, r, l, e : e + count] += part

    def own(step, frame, count, tap):
        y = own_rows(xs[step], (wa, wb)[step], frame, count, tap)
        for r in range(2):
            for l in range(3):
                at = (3 * r + l) * channels
                add(frame, count, r, l, y[:, at : at + channels], tap == 2)

    def halo(step, frame, count, taps):
        for r in range(2):
            y = halo_row(xs[step], (wa, wb)[step], frame, count, r, taps)
            for l in range(3):
                add(frame, count, r, l, y[:, l * channels : (l + 1) * channels], False)

    def summed(f, r):
        pair, e = divmod(f, 2)
        return shift_sum(acc[pair, r, 0, e], acc[pair, r, 1, e], acc[pair, r, 2, e])

    def second(f):
        for r in range(2):
            xb[2 + f, 1 + r] = activate(summed(f, r), gains[1], live[r]).astype(BF16)
        ready(1, 2 + f)

    def finish(f):
        for r in range(2):
            total = lat[f, r].astype(F32) + summed(f, r)
            outv[f, r] = (total * live[r]).astype(BF16)
        out_copy[f].start()

    for f in reversed(range(frames)):
        lat_copy[f].wait()
        for r in range(2):
            xa[2 + f, 1 + r] = activate(lat[f, r].astype(F32), gains[0], live[r]).astype(BF16)
        if f == frames - 1:
            count = sum(there.astype(jnp.int32) for there, _ in around)
            pl.semaphore_wait(barrier, count)
        ready(0, 2 + f)
        if f >= 2:
            wa_copy[f - 2].start()

    for x in xs:

        @pl.when(jnp.logical_not(above))
        def _():
            x[:, 0] = jnp.zeros((frames + 2, columns, channels), BF16)

        @pl.when(jnp.logical_not(below))
        def _():
            x[:, 3] = jnp.zeros((frames + 2, columns, channels), BF16)

        @pl.when(jnp.logical_not(earlier))
        def _():
            x[0:2] = jnp.zeros((2, rows + 2, columns, channels), BF16)

    for tap in (2, 1, 0):
        wa_copy[tap].wait()
        own(0, 2, 2, tap)
        wb_copy[tap].start()
    own(0, 0, 2, 2)
    wait_rows(0, (5, 4))
    halo(0, 2, 2, (2,))
    pass_frame(0, 1)
    own(0, 0, 2, 1)
    wait_rows(0, (3, 2))
    halo(0, 2, 2, (0, 1))
    second(3)
    second(2)
    wb_copy[2].wait()
    own(1, 2, 2, 2)
    own(0, 1, 1, 0)
    pass_frame(0, 0)
    wait_rows(0, (1,))
    halo(0, 0, 2, (1, 2))
    halo(0, 1, 1, (0,))
    second(1)
    wb_copy[1].wait()
    own(1, 2, 2, 1)
    wait_rows(1, (5, 4))
    halo(1, 2, 2, (2,))
    own(0, 0, 1, 0)
    wait_rows(0, (0,))
    halo(0, 0, 1, (0,))
    second(0)

    own(1, 0, 2, 2)
    pass_frame(1, 1)
    wb_copy[0].wait()
    own(1, 2, 2, 0)
    own(1, 0, 2, 1)
    wait_rows(1, (3, 2))
    halo(1, 2, 2, (0, 1))
    finish(3)
    finish(2)
    pass_frame(1, 0)
    wait_rows(1, (1,))
    halo(1, 0, 2, (1, 2))
    own(1, 1, 1, 0)
    halo(1, 1, 1, (0,))
    finish(1)
    own(1, 0, 1, 0)
    wait_rows(1, (0,))
    halo(1, 0, 1, (0,))
    finish(0)

    for copy in out_copy:
        copy.wait()
    for step in range(2):
        for e in range(2):

            @pl.when(later)
            def _():
                to_next(step, e).wait_send()

        for f in range(frames + 2):
            for way, there in enumerate((above, below)):

                @pl.when(along(f, there))
                def _():
                    to_tile(step, way, f).wait_send()


def solution(mesh):
    tiles, groups = mesh.shape["tile"], mesh.shape["group"]

    def local(latent, tile_rows, gain_first, kernel_first, gain_second, kernel_second):
        frames, rows, columns, channels = latent.shape
        halo = (frames + 2, rows + 2, columns, channels)
        vmem = pl.BlockSpec(memory_space=pltpu.VMEM)
        away = pl.BlockSpec(memory_space=pl.ANY)
        smem = pl.BlockSpec(memory_space=pltpu.SMEM)
        dma = pltpu.SemaphoreType.DMA
        return pl.pallas_call(
            functools.partial(kernel, tiles, groups),
            out_shape=jax.ShapeDtypeStruct(latent.shape, BF16),
            in_specs=[away, smem, vmem, away, vmem, away],
            out_specs=away,
            scratch_shapes=[
                pltpu.VMEM(halo, BF16),
                pltpu.VMEM(halo, BF16),
                pltpu.VMEM(kernel_first.shape, BF16),
                pltpu.VMEM(kernel_second.shape, BF16),
                pltpu.VMEM(latent.shape, BF16),
                pltpu.VMEM((2, 2, 3, 2, columns, channels), F32),
                pltpu.VMEM(latent.shape, BF16),
                dma((frames,)),
                dma((6,)),
                dma((frames,)),
                dma((2, 2)),
                dma((2, 2)),
                dma((2, 2, frames + 2)),
                dma((2, 2, frames + 2)),
            ],
            compiler_params=pltpu.CompilerParams(
                collective_id=0, has_side_effects=True, vmem_limit_bytes=56 * 2**20
            ),
            cost_estimate=pl.CostEstimate(
                flops=4 * 27 * frames * rows * columns * channels * channels,
                bytes_accessed=2 * (2 * latent.size + 2 * kernel_first.size),
                transcendentals=2 * latent.size,
            ),
        )(
            latent, tile_rows,
            gain_first, kernel_first,
            gain_second, kernel_second,
        )

    in_specs = (P("group", "tile", None, None), P(), P(), P(), P(), P())
    out_specs = P("group", "tile", None, None)
    return jax.shard_map(local, mesh=mesh, in_specs=in_specs, out_specs=out_specs, check_vma=False)
```

```python
import functools

import jax
import jax.numpy as jnp
from jax import lax
from jax.experimental import pallas as pl
from jax.experimental.pallas import tpu as pltpu
from jax.sharding import PartitionSpec as P

MESH = pl.DeviceIdType.MESH
cat = jnp.concatenate
F32 = jnp.float32
BF16 = jnp.bfloat16


def activate(values, gain, live):
    scale = lax.rsqrt(jnp.mean(values * values, axis=-1, keepdims=True) + 1e-06)
    u = values * scale * gain
    return (u / (1.0 + jnp.exp(-u))) * live


def shift_sum(before, here, after):
    columns = here.shape[0]
    place = lax.broadcasted_iota(jnp.int32, here.shape, 0)
    left = jnp.where(place == 0, 0.0, pltpu.roll(before, 1, 0))
    right = jnp.where(place == columns - 1, 0.0, pltpu.roll(after, columns - 1, 0))
    return left + here + right


def own_rows(x, w, frame, count, tap):
    _, _, columns, channels = x.shape
    at = frame + tap
    lhs = cat([x[at : at + count, r].reshape(count * columns, channels) for r in (1, 2)], axis=1)
    rhs = cat([cat([w[tap, r - out, l] for out in (0, 1) for l in range(3)], axis=1) for r in (1, 2)], axis=0)
    return jnp.dot(lhs, rhs, preferred_element_type=F32)


def halo_row(x, w, frame, count, out, taps):
    _, _, columns, channels = x.shape
    lhs = cat([x[frame + i : frame + i + count, 3 * out].reshape(count * columns, channels) for i in taps], axis=1)
    rhs = cat([cat([w[i, 2 * out, l] for l in range(3)], axis=1) for i in taps], axis=0)
    return jnp.dot(lhs, rhs, preferred_element_type=F32)


def kernel(
    tiles, groups,
    latent, tile_rows, gain_first, kernel_first, gain_second, kernel_second,
    decoded,
    xa, xb, wa, wb, lat, acc,
    lat_sem, w_sem, send_y, recv_y, send_r, recv_r,
):
    frames, rows, columns, channels = lat.shape
    tile = lax.axis_index("tile")
    group = lax.axis_index("group")
    above, below = tile > 0, tile < tiles - 1
    earlier, later = group > 0, group < groups - 1
    up, down = jnp.maximum(tile - 1, 0), jnp.minimum(tile + 1, tiles - 1)
    before, after = jnp.maximum(group - 1, 0), jnp.minimum(group + 1, groups - 1)

    lat_copy = [pltpu.make_async_copy(latent.at[f], lat.at[f], lat_sem.at[f]) for f in range(frames)]
    wa_copy = [pltpu.make_async_copy(kernel_first.at[i], wa.at[i], w_sem.at[i]) for i in range(3)]
    wb_copy = [pltpu.make_async_copy(kernel_second.at[i], wb.at[i], w_sem.at[3 + i]) for i in range(3)]
    for copy in (*lat_copy[::-1], wa_copy[2]):
        copy.start()

    barrier = pltpu.get_barrier_semaphore()
    around = ((above, (up, group)), (below, (down, group)), (earlier, (tile, before)), (later, (tile, after)))
    for there, place in around:

        @pl.when(there)
        def _():
            pl.semaphore_signal(barrier, inc=1, device_id=place, device_id_type=MESH)

    live = [jnp.minimum(jnp.maximum(tile_rows[tile] - r, 0), 1).astype(F32) for r in range(rows)]
    gains = [gain_first[...].reshape(1, channels), gain_second[...].reshape(1, channels)]
    xs = (xa, xb)

    def to_next(step, e):
        x = xs[step]
        return pltpu.make_async_remote_copy(
            src_ref=x.at[frames + e, 1:3], dst_ref=x.at[e, 1:3],
            send_sem=send_y.at[step, e], recv_sem=recv_y.at[step, e],
            device_id=(tile, after), device_id_type=MESH,
        )

    def to_tile(step, way, f):
        x = xs[step]
        source, target = ((1, 3), (2, 0))[way]
        return pltpu.make_async_remote_copy(
            src_ref=x.at[f, source], dst_ref=x.at[f, target],
            send_sem=send_r.at[step, way, f], recv_sem=recv_r.at[step, way, f],
            device_id=((up, down)[way], group), device_id_type=MESH,
        )

    def along(f, there):
        return there if f >= 2 else there & earlier

    def send_rows(step, f):
        for way, there in enumerate((above, below)):

            @pl.when(along(f, there))
            def _():
                to_tile(step, way, f).start()

    def wait_rows(step, fs):
        for f in fs:
            for way, there in enumerate((below, above)):

                @pl.when(along(f, there))
                def _():
                    to_tile(step, way, f).wait_recv()

    def send_frame(step, e):
        @pl.when(later)
        def _():
            to_next(step, e).start()

    def pass_frame(step, e):
        @pl.when(earlier)
        def _():
            to_next(step, e).wait_recv()

        send_rows(step, e)

    def ready(step, f):
        if f >= frames:
            send_frame(step, f - frames)
        send_rows(step, f)

    def add(frame, count, r, l, part, fresh):
        pair, e = divmod(frame, 2)
        part = part.reshape(count, columns, channels)
        if fresh:
            acc[pair, r, l, e : e + count] = part
        else:
            acc[pair, r, l, e : e + count] += part

    def own(step, frame, count, tap):
        y = own_rows(xs[step], (wa, wb)[step], frame, count, tap)
        for r in range(2):
            for l in range(3):
                at = (3 * r + l) * channels
                add(frame, count, r, l, y[:, at : at + channels], tap == 2)

    def halo(step, frame, count, taps):
        for r in range(2):
            y = halo_row(xs[step], (wa, wb)[step], frame, count, r, taps)
            for l in range(3):
                add(frame, count, r, l, y[:, l * channels : (l + 1) * channels], False)

    def summed(f, r):
        pair, e = divmod(f, 2)
        return shift_sum(acc[pair, r, 0, e], acc[pair, r, 1, e], acc[pair, r, 2, e])

    def second(f):
        for r in range(2):
            xb[2 + f, 1 + r] = activate(summed(f, r), gains[1], live[r]).astype(BF16)
        ready(1, 2 + f)

    def finish(f):
        for r in range(2):
            total = lat[f, r].astype(F32) + summed(f, r)
            decoded[f, r] = (total * live[r]).astype(BF16)

    for f in reversed(range(frames)):
        lat_copy[f].wait()
        for r in range(2):
            xa[2 + f, 1 + r] = activate(lat[f, r].astype(F32), gains[0], live[r]).astype(BF16)
        if f == frames - 1:
            count = sum(there.astype(jnp.int32) for there, _ in around)
            pl.semaphore_wait(barrier, count)
        ready(0, 2 + f)
        if f >= 2:
            wa_copy[f - 2].start()

    for x in xs:

        @pl.when(jnp.logical_not(above))
        def _():
            x[:, 0] = jnp.zeros((frames + 2, columns, channels), BF16)

        @pl.when(jnp.logical_not(below))
        def _():
            x[:, 3] = jnp.zeros((frames + 2, columns, channels), BF16)

        @pl.when(jnp.logical_not(earlier))
        def _():
            x[0:2] = jnp.zeros((2, rows + 2, columns, channels), BF16)

    for tap in (2, 1, 0):
        wa_copy[tap].wait()
        own(0, 2, 2, tap)
        wb_copy[tap].start()
    own(0, 0, 2, 2)
    wait_rows(0, (5, 4))
    halo(0, 2, 2, (2,))
    pass_frame(0, 1)
    own(0, 0, 2, 1)
    wait_rows(0, (3, 2))
    halo(0, 2, 2, (0, 1))
    second(3)
    second(2)
    wb_copy[2].wait()
    own(1, 2, 2, 2)
    own(0, 1, 1, 0)
    pass_frame(0, 0)
    wait_rows(0, (1,))
    halo(0, 0, 2, (1, 2))
    halo(0, 1, 1, (0,))
    second(1)
    wb_copy[1].wait()
    own(1, 2, 2, 1)
    wait_rows(1, (5, 4))
    halo(1, 2, 2, (2,))
    own(0, 0, 1, 0)
    wait_rows(0, (0,))
    halo(0, 0, 1, (0,))
    second(0)

    own(1, 0, 2, 2)
    pass_frame(1, 1)
    wb_copy[0].wait()
    own(1, 2, 2, 0)
    own(1, 0, 2, 1)
    pass_frame(1, 0)
    wait_rows(1, (3, 2))
    halo(1, 2, 2, (0, 1))
    finish(3)
    finish(2)
    wait_rows(1, (1,))
    halo(1, 0, 2, (1, 2))
    own(1, 1, 1, 0)
    halo(1, 1, 1, (0,))
    finish(1)
    own(1, 0, 1, 0)
    wait_rows(1, (0,))
    halo(1, 0, 1, (0,))
    finish(0)

    for step in range(2):
        for e in range(2):

            @pl.when(later)
            def _():
                to_next(step, e).wait_send()

        for f in range(frames + 2):
            for way, there in enumerate((above, below)):

                @pl.when(along(f, there))
                def _():
                    to_tile(step, way, f).wait_send()


def solution(mesh):
    tiles, groups = mesh.shape["tile"], mesh.shape["group"]

    def local(latent, tile_rows, gain_first, kernel_first, gain_second, kernel_second):
        frames, rows, columns, channels = latent.shape
        halo = (frames + 2, rows + 2, columns, channels)
        vmem = pl.BlockSpec(memory_space=pltpu.VMEM)
        away = pl.BlockSpec(memory_space=pl.ANY)
        smem = pl.BlockSpec(memory_space=pltpu.SMEM)
        dma = pltpu.SemaphoreType.DMA
        return pl.pallas_call(
            functools.partial(kernel, tiles, groups),
            out_shape=pltpu.VMEM(latent.shape, BF16),
            in_specs=[away, smem, vmem, away, vmem, away],
            out_specs=pl.BlockSpec(memory_space=pltpu.VMEM),
            scratch_shapes=[
                pltpu.VMEM(halo, BF16),
                pltpu.VMEM(halo, BF16),
                pltpu.VMEM(kernel_first.shape, BF16),
                pltpu.VMEM(kernel_second.shape, BF16),
                pltpu.VMEM(latent.shape, BF16),
                pltpu.VMEM((2, 2, 3, 2, columns, channels), F32),
                dma((frames,)),
                dma((6,)),
                dma((2, 2)),
                dma((2, 2)),
                dma((2, 2, frames + 2)),
                dma((2, 2, frames + 2)),
            ],
            compiler_params=pltpu.CompilerParams(
                collective_id=0, has_side_effects=True, vmem_limit_bytes=56 * 2**20
            ),
            cost_estimate=pl.CostEstimate(
                flops=4 * 27 * frames * rows * columns * channels * channels,
                bytes_accessed=2 * (2 * latent.size + 2 * kernel_first.size),
                transcendentals=2 * latent.size,
            ),
        )(
            latent, tile_rows,
            gain_first, kernel_first,
            gain_second, kernel_second,
        )

    in_specs = (P("group", "tile", None, None), P(), P(), P(), P(), P())
    out_specs = P("group", "tile", None, None)
    return jax.shard_map(local, mesh=mesh, in_specs=in_specs, out_specs=out_specs, check_vma=False)
```

```python
import functools

import jax
import jax.numpy as jnp
from jax import lax
from jax.experimental import pallas as pl
from jax.experimental.pallas import tpu as pltpu
from jax.sharding import PartitionSpec as P

MESH = pl.DeviceIdType.MESH
cat = jnp.concatenate
F32 = jnp.float32
BF16 = jnp.bfloat16


def activate(values, gain, live):
    scale = lax.rsqrt(jnp.mean(values * values, axis=-1, keepdims=True) + 1e-06)
    h = values * scale * (0.5 * gain)
    return (h + h * jnp.tanh(h)) * live


def shift_sum(before, here, after):
    columns = here.shape[0]
    place = lax.broadcasted_iota(jnp.int32, here.shape, 0)
    left = jnp.where(place == 0, 0.0, pltpu.roll(before, 1, 0))
    right = jnp.where(place == columns - 1, 0.0, pltpu.roll(after, columns - 1, 0))
    return left + here + right


def own_rows(x, w, frame, count, tap):
    _, _, columns, channels = x.shape
    at = frame + tap
    lhs = cat([x[at : at + count, r].reshape(count * columns, channels) for r in (1, 2)], axis=1)
    rhs = cat([cat([w[tap, r - out, l] for out in (0, 1) for l in range(3)], axis=1) for r in (1, 2)], axis=0)
    return jnp.dot(lhs, rhs, preferred_element_type=F32)


def halo_row(x, w, frame, count, out, taps):
    _, _, columns, channels = x.shape
    lhs = cat([x[frame + i : frame + i + count, 3 * out].reshape(count * columns, channels) for i in taps], axis=1)
    rhs = cat([cat([w[i, 2 * out, l] for l in range(3)], axis=1) for i in taps], axis=0)
    return jnp.dot(lhs, rhs, preferred_element_type=F32)


def kernel(
    tiles, groups,
    latent, tile_rows, gain_first, kernel_first, gain_second, kernel_second,
    decoded,
    xa, xb, wa, wb, lat, acc,
    lat_sem, w_sem, send_y, recv_y, send_r, recv_r,
):
    frames, rows, columns, channels = lat.shape
    tile = lax.axis_index("tile")
    group = lax.axis_index("group")
    above, below = tile > 0, tile < tiles - 1
    earlier, later = group > 0, group < groups - 1
    up, down = jnp.maximum(tile - 1, 0), jnp.minimum(tile + 1, tiles - 1)
    before, after = jnp.maximum(group - 1, 0), jnp.minimum(group + 1, groups - 1)

    lat_copy = [pltpu.make_async_copy(latent.at[f], lat.at[f], lat_sem.at[f]) for f in range(frames)]
    wa_copy = [pltpu.make_async_copy(kernel_first.at[i], wa.at[i], w_sem.at[i]) for i in range(3)]
    wb_copy = [pltpu.make_async_copy(kernel_second.at[i], wb.at[i], w_sem.at[3 + i]) for i in range(3)]
    barrier = pltpu.get_barrier_semaphore()
    around = ((above, (up, group)), (below, (down, group)), (earlier, (tile, before)), (later, (tile, after)))
    for there, place in around:

        @pl.when(there)
        def _():
            pl.semaphore_signal(barrier, inc=1, device_id=place, device_id_type=MESH)

    for copy in (*lat_copy[::-1], wa_copy[2]):
        copy.start()

    live = [jnp.minimum(jnp.maximum(tile_rows[tile] - r, 0), 1).astype(F32) for r in range(rows)]
    gains = [gain_first[...].reshape(1, channels), gain_second[...].reshape(1, channels)]
    xs = (xa, xb)

    def to_next(step, e, count=1):
        x = xs[step]
        return pltpu.make_async_remote_copy(
            src_ref=x.at[frames + e : frames + e + count, 1:3], dst_ref=x.at[e : e + count, 1:3],
            send_sem=send_y.at[step], recv_sem=recv_y.at[step, e],
            device_id=(tile, after), device_id_type=MESH,
        )

    def to_tile(step, way, f, count=1):
        x = xs[step]
        source, target = ((1, 3), (2, 0))[way]
        return pltpu.make_async_remote_copy(
            src_ref=x.at[f : f + count, source], dst_ref=x.at[f : f + count, target],
            send_sem=send_r.at[step, way, min(f // 2, 1)], recv_sem=recv_r.at[step, way, f if f < 2 else 1 + f // 2],
            device_id=((up, down)[way], group), device_id_type=MESH,
        )

    def along(f, there):
        return there if f >= 2 else there & earlier

    def send_rows(step, f):
        for way, there in enumerate((above, below)):

            @pl.when(along(f, there))
            def _():
                to_tile(step, way, f).start()

    def wait_rows(step, fs):
        for way, there in enumerate((below, above)):

            @pl.when(along(fs[-1], there))
            def _():
                to_tile(step, way, fs[-1], len(fs)).wait_recv()

    def send_frame(step, e):
        @pl.when(later)
        def _():
            to_next(step, e).start()

    def pass_frame(step, e):
        @pl.when(earlier)
        def _():
            to_next(step, e).wait_recv()

        send_rows(step, e)

    def ready(step, f):
        if f >= frames:
            send_frame(step, f - frames)
        send_rows(step, f)

    def add(frame, count, r, l, part, fresh):
        pair, e = divmod(frame, 2)
        part = part.reshape(count, columns, channels)
        if fresh:
            acc[pair, r, l, e : e + count] = part
        else:
            acc[pair, r, l, e : e + count] += part

    def own(step, frame, count, tap):
        y = own_rows(xs[step], (wa, wb)[step], frame, count, tap)
        for r in range(2):
            for l in range(3):
                at = (3 * r + l) * channels
                add(frame, count, r, l, y[:, at : at + channels], tap == 2)

    def halo(step, frame, count, taps):
        for r in range(2):
            y = halo_row(xs[step], (wa, wb)[step], frame, count, r, taps)
            for l in range(3):
                add(frame, count, r, l, y[:, l * channels : (l + 1) * channels], False)

    def summed(f, r):
        pair, e = divmod(f, 2)
        return shift_sum(acc[pair, r, 0, e], acc[pair, r, 1, e], acc[pair, r, 2, e])

    def second(f):
        for r in range(2):
            xb[2 + f, 1 + r] = activate(summed(f, r), gains[1], live[r]).astype(BF16)
        ready(1, 2 + f)

    def finish(f):
        for r in range(2):
            total = lat[f, r].astype(F32) + summed(f, r)
            decoded[f, r] = (total * live[r]).astype(BF16)

    for f in reversed(range(frames)):
        lat_copy[f].wait()
        for r in range(2):
            xa[2 + f, 1 + r] = activate(lat[f, r].astype(F32), gains[0], live[r]).astype(BF16)
        if f == frames - 1:
            count = sum(there.astype(jnp.int32) for there, _ in around)
            pl.semaphore_wait(barrier, count)
        ready(0, 2 + f)
        if f >= 2:
            wa_copy[f - 2].start()

    for x in xs:

        @pl.when(jnp.logical_not(above))
        def _():
            x[:, 0] = jnp.zeros((frames + 2, columns, channels), BF16)

        @pl.when(jnp.logical_not(below))
        def _():
            x[:, 3] = jnp.zeros((frames + 2, columns, channels), BF16)

        @pl.when(jnp.logical_not(earlier))
        def _():
            x[0:2] = jnp.zeros((2, rows + 2, columns, channels), BF16)

    for tap in (2, 1, 0):
        wa_copy[tap].wait()
        own(0, 2, 2, tap)
        wb_copy[tap].start()
    own(0, 0, 2, 2)
    wait_rows(0, (5, 4))
    halo(0, 2, 2, (2,))
    pass_frame(0, 1)
    own(0, 0, 2, 1)
    wait_rows(0, (3, 2))
    halo(0, 2, 2, (0, 1))
    second(3)
    second(2)
    wb_copy[2].wait()
    own(1, 2, 2, 2)
    own(0, 1, 1, 0)
    pass_frame(0, 0)
    wait_rows(0, (1,))
    halo(0, 0, 2, (1, 2))
    halo(0, 1, 1, (0,))
    second(1)
    wb_copy[1].wait()
    own(1, 2, 2, 1)
    wait_rows(1, (5, 4))
    halo(1, 2, 2, (2,))
    own(0, 0, 1, 0)
    wait_rows(0, (0,))
    halo(0, 0, 1, (0,))
    second(0)

    own(1, 0, 2, 2)
    pass_frame(1, 1)
    wb_copy[0].wait()
    own(1, 2, 2, 0)
    own(1, 0, 2, 1)
    pass_frame(1, 0)
    wait_rows(1, (3, 2))
    halo(1, 2, 2, (0, 1))
    finish(3)
    finish(2)
    wait_rows(1, (1,))
    halo(1, 0, 2, (1, 2))
    own(1, 1, 1, 0)
    halo(1, 1, 1, (0,))
    finish(1)
    own(1, 0, 1, 0)
    wait_rows(1, (0,))
    halo(1, 0, 1, (0,))
    finish(0)

    for step in range(2):

        @pl.when(later)
        def _():
            to_next(step, 0, 2).wait_send()

        for way, there in enumerate((above, below)):

            @pl.when(there)
            def _():
                to_tile(step, way, 2, frames).wait_send()

            @pl.when(there & earlier)
            def _():
                to_tile(step, way, 0, 2).wait_send()


def solution(mesh):
    tiles, groups = mesh.shape["tile"], mesh.shape["group"]

    def local(latent, tile_rows, gain_first, kernel_first, gain_second, kernel_second):
        frames, rows, columns, channels = latent.shape
        halo = (frames + 2, rows + 2, columns, channels)
        vmem = pl.BlockSpec(memory_space=pltpu.VMEM)
        away = pl.BlockSpec(memory_space=pl.ANY)
        smem = pl.BlockSpec(memory_space=pltpu.SMEM)
        dma = pltpu.SemaphoreType.DMA
        return pl.pallas_call(
            functools.partial(kernel, tiles, groups),
            out_shape=pltpu.VMEM(latent.shape, BF16),
            in_specs=[away, smem, vmem, away, vmem, away],
            out_specs=pl.BlockSpec(memory_space=pltpu.VMEM),
            scratch_shapes=[
                pltpu.VMEM(halo, BF16),
                pltpu.VMEM(halo, BF16),
                pltpu.VMEM(kernel_first.shape, BF16),
                pltpu.VMEM(kernel_second.shape, BF16),
                pltpu.VMEM(latent.shape, BF16),
                pltpu.VMEM((2, 2, 3, 2, columns, channels), F32),
                dma((frames,)),
                dma((6,)),
                dma((2,)),
                dma((2, 2)),
                dma((2, 2, 2)),
                dma((2, 2, 4)),
            ],
            compiler_params=pltpu.CompilerParams(
                collective_id=0, has_side_effects=True, vmem_limit_bytes=56 * 2**20
            ),
            cost_estimate=pl.CostEstimate(
                flops=4 * 27 * frames * rows * columns * channels * channels,
                bytes_accessed=2 * (2 * latent.size + 2 * kernel_first.size),
                transcendentals=2 * latent.size,
            ),
        )(
            latent, tile_rows,
            gain_first, kernel_first,
            gain_second, kernel_second,
        )

    in_specs = (P("group", "tile", None, None), P(), P(), P(), P(), P())
    out_specs = P("group", "tile", None, None)
    return jax.shard_map(local, mesh=mesh, in_specs=in_specs, out_specs=out_specs, check_vma=False)
```

```python
import functools

import jax
import jax.numpy as jnp
from jax import lax
from jax.experimental import pallas as pl
from jax.experimental.pallas import tpu as pltpu
from jax.sharding import PartitionSpec as P

MESH = pl.DeviceIdType.MESH
cat = jnp.concatenate
F32 = jnp.float32
BF16 = jnp.bfloat16


def activate(values, gain, live):
    scale = lax.rsqrt(jnp.mean(values * values, axis=-1, keepdims=True) + 1e-06)
    h = values * scale * (0.5 * gain)
    return (h + h * jnp.tanh(h)) * live


def shift_sum(before, here, after):
    columns = here.shape[0]
    place = lax.broadcasted_iota(jnp.int32, here.shape, 0)
    left = jnp.where(place == 0, 0.0, pltpu.roll(before, 1, 0))
    right = jnp.where(place == columns - 1, 0.0, pltpu.roll(after, columns - 1, 0))
    return left + here + right


def own_rows(x, w, frame, count, tap):
    _, _, columns, channels = x.shape
    at = frame + tap
    lhs = cat([x[at : at + count, r].reshape(count * columns, channels) for r in (1, 2)], axis=1)
    rhs = cat([cat([w[tap, r - out, l] for out in (0, 1) for l in range(3)], axis=1) for r in (1, 2)], axis=0)
    return jnp.dot(lhs, rhs, preferred_element_type=F32)


def halo_row(x, w, frame, count, out, taps):
    _, _, columns, channels = x.shape
    lhs = cat([x[frame + i : frame + i + count, 3 * out].reshape(count * columns, channels) for i in taps], axis=1)
    rhs = cat([cat([w[i, 2 * out, l] for l in range(3)], axis=1) for i in taps], axis=0)
    return jnp.dot(lhs, rhs, preferred_element_type=F32)


def kernel(
    tiles, groups,
    latent, tile_rows, gain_first, kernel_first, gain_second, kernel_second,
    decoded,
    xa, xb, wa, wb, lat, acc,
    lat_sem, w_sem, send_y, recv_y, send_r, recv_r,
):
    frames, rows, columns, channels = lat.shape
    tile = lax.axis_index("tile")
    group = lax.axis_index("group")
    above, below = tile > 0, tile < tiles - 1
    earlier, later = group > 0, group < groups - 1
    up, down = jnp.maximum(tile - 1, 0), jnp.minimum(tile + 1, tiles - 1)
    before, after = jnp.maximum(group - 1, 0), jnp.minimum(group + 1, groups - 1)

    lat_copy = [pltpu.make_async_copy(latent.at[f], lat.at[f], lat_sem.at[f]) for f in range(frames)]
    wa_copy = [pltpu.make_async_copy(kernel_first.at[i], wa.at[i], w_sem.at[i]) for i in range(3)]
    wb_copy = [pltpu.make_async_copy(kernel_second.at[i], wb.at[i], w_sem.at[3 + i]) for i in range(3)]
    barrier = pltpu.get_barrier_semaphore()
    around = ((above, (up, group)), (below, (down, group)), (earlier, (tile, before)), (later, (tile, after)))
    for there, place in around:

        @pl.when(there)
        def _():
            pl.semaphore_signal(barrier, inc=1, device_id=place, device_id_type=MESH)

    for copy in (*lat_copy[::-1], wa_copy[2]):
        copy.start()

    live = [jnp.minimum(jnp.maximum(tile_rows[tile] - r, 0), 1).astype(F32) for r in range(rows)]
    gains = [gain_first[...].reshape(1, channels), gain_second[...].reshape(1, channels)]
    xs = (xa, xb)

    def to_next(step, e, count=1):
        x = xs[step]
        return pltpu.make_async_remote_copy(
            src_ref=x.at[frames + e : frames + e + count, 1:3], dst_ref=x.at[e : e + count, 1:3],
            send_sem=send_y.at[step], recv_sem=recv_y.at[step, e],
            device_id=(tile, after), device_id_type=MESH,
        )

    def to_tile(step, way, f, count=1):
        x = xs[step]
        source, target = ((1, 3), (2, 0))[way]
        return pltpu.make_async_remote_copy(
            src_ref=x.at[f : f + count, source], dst_ref=x.at[f : f + count, target],
            send_sem=send_r.at[step, way, min(f // 2, 1)], recv_sem=recv_r.at[step, way, f if f < 2 else 1 + f // 2],
            device_id=((up, down)[way], group), device_id_type=MESH,
        )

    def along(f, there):
        return there if f >= 2 else there & earlier

    def send_rows(step, f):
        for way, there in enumerate((above, below)):

            @pl.when(along(f, there))
            def _():
                to_tile(step, way, f).start()

    def wait_rows(step, fs):
        for way, there in enumerate((below, above)):

            @pl.when(along(fs[-1], there))
            def _():
                to_tile(step, way, fs[-1], len(fs)).wait_recv()

    def send_frame(step, e):
        @pl.when(later)
        def _():
            to_next(step, e).start()

    def pass_frame(step, e):
        @pl.when(earlier)
        def _():
            to_next(step, e).wait_recv()

        send_rows(step, e)

    def ready(step, f):
        if f >= frames:
            send_frame(step, f - frames)
        send_rows(step, f)

    def add(frame, count, r, l, part, fresh):
        pair, e = divmod(frame, 2)
        part = part.reshape(count, columns, channels)
        if fresh:
            acc[pair, r, l, e : e + count] = part
        else:
            acc[pair, r, l, e : e + count] += part

    def own(step, frame, count, tap):
        y = own_rows(xs[step], (wa, wb)[step], frame, count, tap)
        for r in range(2):
            for l in range(3):
                at = (3 * r + l) * channels
                add(frame, count, r, l, y[:, at : at + channels], tap == 2)

    def halo(step, frame, count, taps):
        for r in range(2):
            y = halo_row(xs[step], (wa, wb)[step], frame, count, r, taps)
            for l in range(3):
                add(frame, count, r, l, y[:, l * channels : (l + 1) * channels], False)

    def summed(f, r):
        pair, e = divmod(f, 2)
        return shift_sum(acc[pair, r, 0, e], acc[pair, r, 1, e], acc[pair, r, 2, e])

    def second(f):
        for r in range(2):
            xb[2 + f, 1 + r] = activate(summed(f, r), gains[1], live[r]).astype(BF16)
        ready(1, 2 + f)

    def finish(f):
        for r in range(2):
            total = lat[f, r].astype(F32) + summed(f, r)
            decoded[f, r] = (total * live[r]).astype(BF16)

    for f in reversed(range(frames)):
        lat_copy[f].wait()
        for r in range(2):
            xa[2 + f, 1 + r] = activate(lat[f, r].astype(F32), gains[0], live[r]).astype(BF16)
        if f == frames - 1:
            count = sum(there.astype(jnp.int32) for there, _ in around)
            pl.semaphore_wait(barrier, count)
        ready(0, 2 + f)
        if f >= 2:
            wa_copy[f - 2].start()

    for x in xs:

        @pl.when(jnp.logical_not(above))
        def _():
            x[:, 0] = jnp.zeros((frames + 2, columns, channels), BF16)

        @pl.when(jnp.logical_not(below))
        def _():
            x[:, 3] = jnp.zeros((frames + 2, columns, channels), BF16)

        @pl.when(jnp.logical_not(earlier))
        def _():
            x[0:2] = jnp.zeros((2, rows + 2, columns, channels), BF16)

    for tap in (2, 1, 0):
        wa_copy[tap].wait()
        own(0, 2, 2, tap)
        wb_copy[tap].start()
    own(0, 0, 2, 2)
    wait_rows(0, (5, 4))
    halo(0, 2, 2, (2,))
    pass_frame(0, 1)
    own(0, 0, 2, 1)
    wait_rows(0, (3, 2))
    halo(0, 2, 2, (0, 1))
    second(3)
    second(2)
    wb_copy[2].wait()
    own(1, 2, 2, 2)
    own(0, 1, 1, 0)
    pass_frame(0, 0)
    wait_rows(0, (1,))
    halo(0, 0, 2, (1, 2))
    halo(0, 1, 1, (0,))
    second(1)
    wb_copy[1].wait()
    own(1, 2, 2, 1)
    wait_rows(1, (5, 4))
    halo(1, 2, 2, (2,))
    own(0, 0, 1, 0)
    wait_rows(0, (0,))
    halo(0, 0, 1, (0,))
    second(0)

    own(1, 0, 2, 2)
    pass_frame(1, 1)
    wb_copy[0].wait()
    own(1, 2, 2, 0)
    own(1, 0, 2, 1)
    pass_frame(1, 0)
    wait_rows(1, (3, 2))
    halo(1, 2, 2, (0, 1))
    wait_rows(1, (1,))
    finish(3)
    halo(1, 0, 2, (1, 2))
    finish(2)
    own(1, 1, 1, 0)
    halo(1, 1, 1, (0,))
    finish(1)
    own(1, 0, 1, 0)
    wait_rows(1, (0,))
    halo(1, 0, 1, (0,))
    finish(0)

    for step in range(2):

        @pl.when(later)
        def _():
            to_next(step, 0, 2).wait_send()

        for way, there in enumerate((above, below)):

            @pl.when(there)
            def _():
                to_tile(step, way, 2, frames).wait_send()

            @pl.when(there & earlier)
            def _():
                to_tile(step, way, 0, 2).wait_send()


def solution(mesh):
    tiles, groups = mesh.shape["tile"], mesh.shape["group"]

    def local(latent, tile_rows, gain_first, kernel_first, gain_second, kernel_second):
        frames, rows, columns, channels = latent.shape
        halo = (frames + 2, rows + 2, columns, channels)
        vmem = pl.BlockSpec(memory_space=pltpu.VMEM)
        away = pl.BlockSpec(memory_space=pl.ANY)
        smem = pl.BlockSpec(memory_space=pltpu.SMEM)
        dma = pltpu.SemaphoreType.DMA
        return pl.pallas_call(
            functools.partial(kernel, tiles, groups),
            out_shape=pltpu.VMEM(latent.shape, BF16),
            in_specs=[away, smem, vmem, away, vmem, away],
            out_specs=pl.BlockSpec(memory_space=pltpu.VMEM),
            scratch_shapes=[
                pltpu.VMEM(halo, BF16),
                pltpu.VMEM(halo, BF16),
                pltpu.VMEM(kernel_first.shape, BF16),
                pltpu.VMEM(kernel_second.shape, BF16),
                pltpu.VMEM(latent.shape, BF16),
                pltpu.VMEM((2, 2, 3, 2, columns, channels), F32),
                dma((frames,)),
                dma((6,)),
                dma((2,)),
                dma((2, 2)),
                dma((2, 2, 2)),
                dma((2, 2, 4)),
            ],
            compiler_params=pltpu.CompilerParams(
                collective_id=0, has_side_effects=True, vmem_limit_bytes=56 * 2**20
            ),
            cost_estimate=pl.CostEstimate(
                flops=4 * 27 * frames * rows * columns * channels * channels,
                bytes_accessed=2 * (2 * latent.size + 2 * kernel_first.size),
                transcendentals=2 * latent.size,
            ),
        )(
            latent, tile_rows,
            gain_first, kernel_first,
            gain_second, kernel_second,
        )

    in_specs = (P("group", "tile", None, None), P(), P(), P(), P(), P())
    out_specs = P("group", "tile", None, None)
    return jax.shard_map(local, mesh=mesh, in_specs=in_specs, out_specs=out_specs, check_vma=False)
```
